256 devices in a mesh: rep: 16 (over x_lo, y, core), et: 16 (over z, x_hi).
Axes of the slice: x: 4 (x_hi: 2, x_lo: 2; x = x_hi * 2 + x_lo), y: 4, z: 8, core: 2. Of those that a mesh axis runs over, the one named last changes fastest.
Arguments:
- tokens: bfloat16 [32768, 2048], P(('rep', 'et')), parts along dimension 0, may hold values from -6 to 6
- expert_ids: int32 [32768, 2], P(('rep', 'et')), parts along dimension 0, may hold values from 0 to 7, as said below
- route_logits: float32 [32768, 2], P(('rep', 'et')), parts along dimension 0, may hold values from -3 to 3
- w_gate: bfloat16 [2, 7168, 2048], P(None, 'et'), may hold values from -0.125 to 0.125
- w_up: bfloat16 [2, 7168, 2048], P(None, 'et'), may hold values from -0.125 to 0.125
- w_down: bfloat16 [2, 7168, 2048], P(None, 'et'), may hold values from -0.0625 to 0.0625
Outputs:
- mixed: bfloat16 [32768, 2048], P(('rep', 'et')), parts along dimension 0
The draws below stay inside these ranges and needn't reach their ends.
There are 16 independent parts, one for each index of `rep`. The reference program is written for one: setup_inputs(seed, part) draws one part's arguments, and reference() takes and returns one part's arrays. A program takes and returns all parts, laid end to end along the dimension named above; an argument that names none is the same for every part. Nothing has to cross between parts.
Inputs may be any that keep to these rules, and one draw needn't show every extreme that they name: `expert_ids`: each row names two different experts. Within each aligned block of 128 rows (the rows of one device), no expert is named by more than 48 rows, and experts 0 and 1 are each named by exactly 48 rows.
All inputs are finite; a program needn't handle non-finite values.
Results may differ from the reference program's by a relative error of at most 0.015.
Values may be sent and summed in bfloat16 or wider, within the bound.
No kernel may reach another device: no remote copies, remote signals or barrier semaphores. Data moves between devices by JAX's collectives and lax.ppermute only.
A program may use at most 128 MiB of HBM per device.

```python
import jax
import jax.numpy as jnp
from jax import lax

D = 2048
FF = 7168
EXPERTS = 8
EXP_WIN = 2
TOK_DEV = 128
CAP = 48
TOKENS = 2048
N_ET = 16


def route_block(key):
    key_order, key_rank, key_rows, key_flip = jax.random.split(key, 4)
    order = jax.random.permutation(key_order, EXPERTS).astype(jnp.int32)
    others = EXPERTS - 2
    remaining = 2 * TOK_DEV - 2 * CAP
    base_count = remaining // others
    extra_count = remaining % others
    other_rank = jax.random.permutation(key_rank, others).astype(jnp.int32)
    numbers = jnp.arange(EXPERTS, dtype=jnp.int32)
    rank_of = other_rank[jnp.clip(numbers - 2, 0, others - 1)]
    counts_by_id = jnp.where(numbers < 2, jnp.int32(CAP), base_count + (rank_of < extra_count).astype(jnp.int32))
    counts_in_order = counts_by_id[order]
    ends = jnp.cumsum(counts_in_order).astype(jnp.int32)
    positions = jnp.arange(2 * TOK_DEV, dtype=jnp.int32)
    group_index = jnp.sum((positions[:, None] >= ends[None, :]).astype(jnp.int32), axis=1)
    labels = order[group_index]
    pairs = jnp.stack([labels[:TOK_DEV], labels[TOK_DEV:]], axis=1)
    row_order = jax.random.permutation(key_rows, TOK_DEV).astype(jnp.int32)
    pairs = pairs[row_order]
    flips = jax.random.randint(key_flip, (TOK_DEV,), 0, 2)
    pairs = jnp.where(flips[:, None] == 1, pairs[:, ::-1], pairs)
    return pairs.astype(jnp.int32)


def draw_expert_ids(key, part):
    key = jax.random.fold_in(key, 11)
    blocks = TOKENS // TOK_DEV
    block_keys = jax.random.split(key, blocks)
    pairs = jax.vmap(route_block)(block_keys)
    return pairs.reshape(TOKENS, 2).astype(jnp.int32)


def levels(rng, shape, cuts, least, largest):
    level, own = 1.0, jax.random.fold_in(rng, 6)
    for position, parts in cuts:
        draws = jnp.exp(jax.random.uniform(jax.random.fold_in(own, position), (parts,), jnp.float32, least / len(cuts), largest / len(cuts)))
        level = level * jnp.repeat(draws, shape[position] // parts).reshape([-1 if axis == position else 1 for axis in range(len(shape))])
    return level


def centred(key, shape, deviation, most, cuts=(), kind=jnp.bfloat16):
    values = jax.random.normal(key, shape, jnp.float32) * deviation
    if len(cuts) > 0:
        values = levels(key, shape, cuts, -0.22, 0.18) * values
    return jnp.clip(values, min=-most, max=most).astype(kind)


def setup_inputs(seed: int = 0, part: int = 0) -> dict:
    splits = jax.random.split(jax.random.key(seed), 7)
    own_keys = jax.random.split(jax.random.fold_in(splits[6], part), 7)
    return {
        "tokens": centred(own_keys[0], (TOKENS, D), 1.0, 6.0, ((0, 16),)),
        "expert_ids": draw_expert_ids(jax.random.fold_in(jax.random.fold_in(splits[6], part), 71), part),
        "route_logits": centred(own_keys[2], (TOKENS, 2), 0.5, 3.0, ((0, 16),), jnp.float32),
        "w_gate": centred(splits[3], (EXP_WIN, FF, D), D ** -0.5, 0.125, ((1, 16),)),
        "w_up": centred(splits[4], (EXP_WIN, FF, D), D ** -0.5, 0.125, ((1, 16),)),
        "w_down": centred(splits[5], (EXP_WIN, FF, D), FF ** -0.5, 0.0625, ((1, 16),)),
    }


def reference(tokens, expert_ids, route_logits, w_gate, w_up, w_down):
    route_probs = jax.nn.softmax(route_logits.astype(jnp.float32), axis=-1).astype(jnp.bfloat16)
    probs_wide = route_probs.astype(jnp.float32)
    limit = N_ET * CAP
    block_units = FF // N_ET
    result = jnp.zeros((tokens.shape[0], tokens.shape[1]), jnp.float32)
    for expert in range(EXP_WIN):
        chosen = expert_ids == expert
        combine = jnp.sum(jnp.where(chosen, probs_wide, jnp.float32(0.0)), axis=-1)
        routed = jnp.any(chosen, axis=-1)
        routed_count = jnp.sum(routed.astype(jnp.int32))
        picks = jnp.nonzero(routed, size=limit, fill_value=0)[0].astype(jnp.int32)
        in_use = jnp.arange(limit, dtype=jnp.int32) < routed_count
        slot_weight = jnp.where(in_use, combine[picks], jnp.float32(0.0))
        picked = tokens[picks].astype(jnp.float32)
        gate_act = jnp.dot(picked, w_gate[expert].astype(jnp.float32).T, precision=lax.Precision.HIGHEST)
        up_act = jnp.dot(picked, w_up[expert].astype(jnp.float32).T, precision=lax.Precision.HIGHEST)
        hidden = (jax.nn.silu(gate_act) * up_act).astype(jnp.bfloat16)
        hidden = lax.optimization_barrier(hidden).astype(jnp.float32)
        hidden_blocks = hidden.reshape(limit, N_ET, block_units)
        down_blocks = w_down[expert].astype(jnp.float32).reshape(N_ET, block_units, tokens.shape[1])
        block_out = jnp.einsum("lnf,nfd->lnd", hidden_blocks, down_blocks, precision=lax.Precision.HIGHEST)
        term = (slot_weight[:, None, None] * block_out).astype(jnp.bfloat16)
        term = lax.optimization_barrier(term).astype(jnp.float32)
        result = result.at[picks].add(jnp.sum(term, axis=1))
    return result.astype(jnp.bfloat16)
```

```python
import jax
import jax.numpy as jnp
from jax import lax
from jax.experimental import pallas as pl
from jax.experimental.pallas import tpu as pltpu
from jax.sharding import Mesh
from jax.sharding import PartitionSpec as P

EXPERTS = 2
CAP = 48
PLANE = ("xl", "y", "xh")
VMEM = 50 * 1024 * 1024


def role_of(index):
    return (index // 2) % 2


def selector(ids, rows):
    chosen = [jnp.any(ids == e, axis=1, keepdims=True) for e in range(EXPERTS)]
    flags = jnp.concatenate([c.astype(jnp.float32) for c in chosen], axis=1)
    before = lax.broadcasted_iota(jnp.int32, (rows, rows), 1) < lax.broadcasted_iota(
        jnp.int32, (rows, rows), 0
    )
    rank = jnp.dot(before.astype(jnp.float32), flags, preferred_element_type=jnp.float32)
    slots = lax.broadcasted_iota(jnp.int32, (rows, CAP), 1).astype(jnp.float32)
    return [(rank[:, e : e + 1] == slots) & chosen[e] for e in range(EXPERTS)]


def pick_kernel(ids_ref, tokens_ref, out_ref):
    tokens = tokens_ref[...]
    marks = selector(ids_ref[...], tokens.shape[0])
    for e in range(EXPERTS):
        picked = lax.dot_general(
            marks[e].astype(jnp.bfloat16),
            tokens,
            (((0,), (0,)), ((), ())),
            preferred_element_type=jnp.float32,
        ).astype(jnp.bfloat16)
        for k in range(out_ref.shape[0]):
            if role_of(k) == e:
                out_ref[k] = picked


def pick(ids, tokens, chips):
    return pl.pallas_call(
        pick_kernel,
        out_shape=jax.ShapeDtypeStruct((chips, CAP, tokens.shape[1]), tokens.dtype),
        compiler_params=pltpu.CompilerParams(vmem_limit_bytes=VMEM),
        name="pick_rows",
    )(ids, tokens)


def pack_kernel(at_ref, gate_ref, up_ref, down_ref, out_ref, sems):
    _, rows, cols = out_ref.shape
    start = pl.multiple_of(at_ref[1] * rows, rows)
    left = pl.multiple_of(at_ref[2] * cols, cols)
    copies = [
        pltpu.make_async_copy(
            ref.at[at_ref[0], pl.ds(start, rows), pl.ds(left, cols)], out_ref.at[n], sems.at[n]
        )
        for n, ref in enumerate((gate_ref, up_ref, down_ref))
    ]
    for copy in copies:
        copy.start()
    for copy in copies:
        copy.wait()


def pack(at, w_gate, w_up, w_down, rows, cols):
    anywhere = pl.BlockSpec(memory_space=pl.ANY)
    return pl.pallas_call(
        pack_kernel,
        out_shape=jax.ShapeDtypeStruct((3, rows, cols), w_gate.dtype),
        in_specs=[pl.BlockSpec(memory_space=pltpu.SMEM)] + [anywhere] * 3,
        out_specs=anywhere,
        scratch_shapes=[pltpu.SemaphoreType.DMA((3,))],
        name="pack_weights",
    )(at, w_gate, w_up, w_down)


def ffn_kernel(
    core_ref,
    x_own,
    x_other,
    gate_own,
    gate_other,
    up_own,
    up_other,
    down_own,
    down_other,
    out_ref,
    hidden,
):
    step = pl.program_id(0)
    chunks = hidden.shape[0]

    def flat(ref, first, count):
        rows, cols = ref.shape[2:]
        return ref[first : first + count, 0].reshape(count * rows, cols)

    def project(own, other):
        dims = (((1,), (1,)), ((), ()))
        count = own.shape[0]
        return lax.dot_general(
            x_own[...], flat(own, 0, count), dims, preferred_element_type=jnp.float32
        ) + lax.dot_general(
            x_other[...], flat(other, 0, count), dims, preferred_element_type=jnp.float32
        )

    def expand(down_ref):
        count = down_ref.shape[0] // chunks
        total = None
        for c in range(chunks):
            part = jnp.dot(
                hidden[c], flat(down_ref, c * count, count), preferred_element_type=jnp.float32
            )
            total = part if total is None else total + part
        out_ref[...] = total.astype(out_ref.dtype)

    @pl.when(step < chunks)
    def _():
        gate = project(gate_own, gate_other)
        up = project(up_own, up_other)
        hidden[step] = (gate / (1.0 + jnp.exp(-gate)) * up).astype(hidden.dtype)

    last_own = chunks + (pl.num_programs(0) - chunks) // 2

    @pl.when((step >= chunks) & (step < last_own))
    def _():
        expand(down_own)

    @pl.when(step >= last_own)
    def _():
        expand(down_other)


def ffn(core, rows, own, other):
    count, width = rows.shape
    depth, _, share, half = own.shape
    chunks = 4
    tiles = 2
    each = depth // chunks

    def side(s, c):
        return jnp.where(s < chunks + tiles, c[0], 1 - c[0])

    def chunk(kind):
        return pl.BlockSpec(
            (each, 1, share, half), lambda s, c: (jnp.minimum(s, chunks - 1), kind, 0, 0)
        )

    def columns(first):
        return pl.BlockSpec(
            (depth, 1, share, half // tiles),
            lambda s, c: (0, 2, 0, jnp.clip(s - first, 0, tiles - 1)),
        )

    return pl.pallas_call(
        ffn_kernel,
        grid_spec=pltpu.PrefetchScalarGridSpec(
            num_scalar_prefetch=1,
            grid=(chunks + 2 * tiles,),
            in_specs=[
                pl.BlockSpec((count, half), lambda s, c: (0, c[0])),
                pl.BlockSpec((count, half), lambda s, c: (0, 1 - c[0])),
                chunk(0),
                chunk(0),
                chunk(1),
                chunk(1),
                columns(chunks),
                columns(chunks + tiles),
            ],
            out_specs=pl.BlockSpec(
                (count, half // tiles),
                lambda s, c: (0, side(s, c) * tiles + jnp.maximum(s - chunks, 0) % tiles),
            ),
            scratch_shapes=[pltpu.VMEM((chunks, count, each * share), rows.dtype)],
        ),
        out_shape=jax.ShapeDtypeStruct((count, width), rows.dtype),
        compiler_params=pltpu.CompilerParams(vmem_limit_bytes=VMEM),
        name="expert_ffn",
    )(core, rows, rows, own, other, own, other, own, other)


def body(tokens, expert_ids, route_logits, w_gate, w_up, w_down):
    width = tokens.shape[1]
    chips = lax.axis_size(PLANE)
    share = w_gate.shape[1] // 4
    half = width // 2
    xl, y, core = lax.axis_index("xl"), lax.axis_index("y"), lax.axis_index("c")
    at = jnp.stack([y % 2, xl * 2 + y // 2, core]).astype(jnp.int32)

    own = lax.all_gather(pack(at, w_gate, w_up, w_down, share, half), "z", axis=0, tiled=False)
    rows = lax.all_to_all(pick(expert_ids, tokens, chips), PLANE, 0, 0)
    rows = rows.reshape(chips * CAP, width)
    own, rows = lax.optimization_barrier((own, rows))
    other = lax.ppermute(own, "c", [(0, 1), (1, 0)])
    partial = ffn(core.astype(jnp.int32).reshape(1), rows, own, other)
    back = lax.all_to_all(partial.reshape(chips, CAP, width), PLANE, 0, 0)
    return mix(expert_ids, route_logits, back)


def mix_kernel(ids_ref, logits_ref, back_ref, out_ref):
    logits = logits_ref[...]
    top = jnp.max(logits, axis=1, keepdims=True)
    powers = jnp.exp(logits - top)
    probs = (powers / jnp.sum(powers, axis=1, keepdims=True)).astype(jnp.bfloat16)
    probs = probs.astype(jnp.float32)
    ids = ids_ref[...]
    marks = selector(ids, logits.shape[0])
    total = None
    for e in range(EXPERTS):
        combine = jnp.sum(jnp.where(ids == e, probs, 0.0), axis=1, keepdims=True)
        place = jnp.where(marks[e], combine, 0.0).astype(jnp.bfloat16)
        value = None
        for k in range(back_ref.shape[0]):
            if role_of(k) == e:
                term = back_ref[k].astype(jnp.float32)
                value = term if value is None else value + term
        high = value.astype(jnp.bfloat16)
        low = (value - high.astype(jnp.float32)).astype(jnp.bfloat16)
        part = jnp.dot(place, high, preferred_element_type=jnp.float32) + jnp.dot(
            place, low, preferred_element_type=jnp.float32
        )
        total = part if total is None else total + part
    out_ref[...] = total.astype(out_ref.dtype)


def mix(ids, logits, back):
    rows = ids.shape[0]
    chips, cap, width = back.shape
    tile = 512
    return pl.pallas_call(
        mix_kernel,
        grid=(width // tile,),
        in_specs=[
            pl.BlockSpec((rows, 2), lambda i: (0, 0)),
            pl.BlockSpec((rows, 2), lambda i: (0, 0)),
            pl.BlockSpec((chips, cap, tile), lambda i: (0, 0, i)),
        ],
        out_specs=pl.BlockSpec((rows, tile), lambda i: (0, i)),
        out_shape=jax.ShapeDtypeStruct((rows, width), back.dtype),
        compiler_params=pltpu.CompilerParams(vmem_limit_bytes=VMEM),
        name="mix_terms",
    )(ids, logits, back)


def solution(mesh):
    fine = Mesh(mesh.devices.reshape(2, 4, 2, 8, 2), ("xl", "y", "c", "z", "xh"))
    tokens = P(("xl", "y", "c", "z", "xh"), None)
    weights = P(None, ("z", "xh"), None)
    return jax.shard_map(
        body,
        mesh=fine,
        in_specs=(tokens,) * 3 + (weights,) * 3,
        out_specs=tokens,
        check_vma=False,
    )
```

```python
import jax
import jax.numpy as jnp
from jax import lax
from jax.experimental import pallas as pl
from jax.experimental.pallas import tpu as pltpu
from jax.sharding import Mesh
from jax.sharding import PartitionSpec as P

EXPERTS = 2
CAP = 48
PLANE = ("xl", "y", "xh")
VMEM = 60 * 1024 * 1024


def role_of(index):
    return (index // 2) % 2


def selector(ids, rows):
    chosen = [jnp.any(ids == e, axis=1, keepdims=True) for e in range(EXPERTS)]
    flags = jnp.concatenate([c.astype(jnp.float32) for c in chosen], axis=1)
    before = lax.broadcasted_iota(jnp.int32, (rows, rows), 1) < lax.broadcasted_iota(
        jnp.int32, (rows, rows), 0
    )
    rank = jnp.dot(before.astype(jnp.float32), flags, preferred_element_type=jnp.float32)
    slots = lax.broadcasted_iota(jnp.int32, (rows, CAP), 1).astype(jnp.float32)
    return [(rank[:, e : e + 1] == slots) & chosen[e] for e in range(EXPERTS)]


def pick_kernel(ids_ref, logits_ref, tokens_ref, out_ref, place_ref):
    tokens = tokens_ref[...]
    ids = ids_ref[...]
    logits = logits_ref[...]
    top = jnp.max(logits, axis=1, keepdims=True)
    powers = jnp.exp(logits - top)
    probs = (powers / jnp.sum(powers, axis=1, keepdims=True)).astype(jnp.bfloat16)
    probs = probs.astype(jnp.float32)
    marks = selector(ids, tokens.shape[0])
    for e in range(EXPERTS):
        combine = jnp.sum(jnp.where(ids == e, probs, 0.0), axis=1, keepdims=True)
        place_ref[e] = jnp.where(marks[e], combine, 0.0).astype(place_ref.dtype)
        picked = lax.dot_general(
            marks[e].astype(jnp.bfloat16),
            tokens,
            (((0,), (0,)), ((), ())),
            preferred_element_type=jnp.float32,
        ).astype(jnp.bfloat16)
        for k in range(out_ref.shape[0]):
            if role_of(k) == e:
                out_ref[k] = picked


def pick(ids, logits, tokens, chips):
    count, width = tokens.shape
    return pl.pallas_call(
        pick_kernel,
        out_shape=[
            jax.ShapeDtypeStruct((chips, CAP, width), tokens.dtype),
            jax.ShapeDtypeStruct((EXPERTS, count, CAP), tokens.dtype),
        ],
        compiler_params=pltpu.CompilerParams(vmem_limit_bytes=VMEM),
        name="pick_rows",
    )(ids, logits, tokens)


def pack_kernel(at_ref, gate_ref, up_ref, down_ref, out_ref, sems):
    _, rows, cols = out_ref.shape
    start = pl.multiple_of(at_ref[1] * rows, rows)
    left = pl.multiple_of(at_ref[2] * cols, cols)
    copies = [
        pltpu.make_async_copy(
            ref.at[at_ref[0], pl.ds(start, rows), pl.ds(left, cols)], out_ref.at[n], sems.at[n]
        )
        for n, ref in enumerate((gate_ref, up_ref, down_ref))
    ]
    for copy in copies:
        copy.start()
    for copy in copies:
        copy.wait()


def pack(at, w_gate, w_up, w_down, rows, cols):
    anywhere = pl.BlockSpec(memory_space=pl.ANY)
    return pl.pallas_call(
        pack_kernel,
        out_shape=jax.ShapeDtypeStruct((3, rows, cols), w_gate.dtype),
        in_specs=[pl.BlockSpec(memory_space=pltpu.SMEM)] + [anywhere] * 3,
        out_specs=pl.BlockSpec(memory_space=pltpu.VMEM),
        scratch_shapes=[pltpu.SemaphoreType.DMA((3,))],
        name="pack_weights",
    )(at, w_gate, w_up, w_down)


def ffn_kernel(
    core_ref,
    x_own,
    x_other,
    gate_own,
    gate_other,
    up_own,
    up_other,
    down_own,
    down_other,
    out_ref,
    hidden,
):
    step = pl.program_id(0)
    chunks = hidden.shape[0]

    def flat(ref, first, count):
        rows, cols = ref.shape[2:]
        return ref[first : first + count, 0].reshape(count * rows, cols)

    def project(own, other):
        dims = (((1,), (1,)), ((), ()))
        count = own.shape[0]
        return lax.dot_general(
            x_own[...], flat(own, 0, count), dims, preferred_element_type=jnp.float32
        ) + lax.dot_general(
            x_other[...], flat(other, 0, count), dims, preferred_element_type=jnp.float32
        )

    def expand(down_ref):
        count = down_ref.shape[0] // chunks
        total = None
        for c in range(chunks):
            part = jnp.dot(
                hidden[c], flat(down_ref, c * count, count), preferred_element_type=jnp.float32
            )
            total = part if total is None else total + part
        out_ref[...] = total.astype(out_ref.dtype)

    @pl.when(step < chunks)
    def _():
        gate = project(gate_own, gate_other)
        up = project(up_own, up_other)
        hidden[step] = (gate / (1.0 + jnp.exp(-gate)) * up).astype(hidden.dtype)

    last_own = chunks + (pl.num_programs(0) - chunks) // 2

    @pl.when((step >= chunks) & (step < last_own))
    def _():
        expand(down_own)

    @pl.when(step >= last_own)
    def _():
        expand(down_other)


def ffn(core, rows, own, other):
    count, width = rows.shape
    depth, _, share, half = own.shape
    chunks = 4
    tiles = 2
    each = depth // chunks

    def side(s, c):
        return jnp.where(s < chunks + tiles, c[0], 1 - c[0])

    def chunk(kind):
        return pl.BlockSpec(
            (each, 1, share, half), lambda s, c: (jnp.minimum(s, chunks - 1), kind, 0, 0)
        )

    def columns(first):
        return pl.BlockSpec(
            (depth, 1, share, half // tiles),
            lambda s, c: (0, 2, 0, jnp.clip(s - first, 0, tiles - 1)),
        )

    return pl.pallas_call(
        ffn_kernel,
        grid_spec=pltpu.PrefetchScalarGridSpec(
            num_scalar_prefetch=1,
            grid=(chunks + 2 * tiles,),
            in_specs=[
                pl.BlockSpec((count, half), lambda s, c: (0, c[0])),
                pl.BlockSpec((count, half), lambda s, c: (0, 1 - c[0])),
                chunk(0),
                chunk(0),
                chunk(1),
                chunk(1),
                columns(chunks),
                columns(chunks + tiles),
            ],
            out_specs=pl.BlockSpec(
                (count, half // tiles),
                lambda s, c: (0, side(s, c) * tiles + jnp.maximum(s - chunks, 0) % tiles),
            ),
            scratch_shapes=[pltpu.VMEM((chunks, count, each * share), rows.dtype)],
        ),
        out_shape=jax.ShapeDtypeStruct((count, width), rows.dtype),
        compiler_params=pltpu.CompilerParams(vmem_limit_bytes=VMEM),
        name="expert_ffn",
    )(core, rows, rows, own, other, own, other, own, other)


def body(tokens, expert_ids, route_logits, w_gate, w_up, w_down):
    width = tokens.shape[1]
    chips = lax.axis_size(PLANE)
    share = w_gate.shape[1] // 4
    half = width // 2
    xl, y, core = lax.axis_index("xl"), lax.axis_index("y"), lax.axis_index("c")
    at = jnp.stack([y % 2, xl * 2 + y // 2, core]).astype(jnp.int32)

    own = lax.all_gather(pack(at, w_gate, w_up, w_down, share, half), "z", axis=0, tiled=False)
    picked, place = pick(expert_ids, route_logits, tokens, chips)
    rows = lax.all_to_all(picked, PLANE, 0, 0)
    rows = rows.reshape(chips * CAP, width)
    own, rows = lax.optimization_barrier((own, rows))
    other = lax.ppermute(own, "c", [(0, 1), (1, 0)])
    partial = ffn(core.astype(jnp.int32).reshape(1), rows, own, other)
    back = lax.all_to_all(partial.reshape(chips, CAP, width), PLANE, 0, 0)
    return mix(place, back)


def mix_kernel(place_ref, back_ref, out_ref):
    total = None
    for e in range(EXPERTS):
        value = None
        for k in range(back_ref.shape[0]):
            if role_of(k) == e:
                term = back_ref[k].astype(jnp.float32)
                value = term if value is None else value + term
        high = value.astype(jnp.bfloat16)
        low = (value - high.astype(jnp.float32)).astype(jnp.bfloat16)
        part = jnp.dot(place_ref[e], high, preferred_element_type=jnp.float32) + jnp.dot(
            place_ref[e], low, preferred_element_type=jnp.float32
        )
        total = part if total is None else total + part
    out_ref[...] = total.astype(out_ref.dtype)


def mix(place, back):
    chips, cap, width = back.shape
    rows = place.shape[1]
    tile = 512
    return pl.pallas_call(
        mix_kernel,
        grid=(width // tile,),
        in_specs=[
            pl.BlockSpec(place.shape, lambda i: (0, 0, 0)),
            pl.BlockSpec((chips, cap, tile), lambda i: (0, 0, i)),
        ],
        out_specs=pl.BlockSpec((rows, tile), lambda i: (0, i)),
        out_shape=jax.ShapeDtypeStruct((rows, width), back.dtype),
        compiler_params=pltpu.CompilerParams(vmem_limit_bytes=VMEM),
        name="mix_terms",
    )(place, back)


def solution(mesh):
    fine = Mesh(mesh.devices.reshape(2, 4, 2, 8, 2), ("xl", "y", "c", "z", "xh"))
    tokens = P(("xl", "y", "c", "z", "xh"), None)
    weights = P(None, ("z", "xh"), None)
    return jax.shard_map(
        body,
        mesh=fine,
        in_specs=(tokens,) * 3 + (weights,) * 3,
        out_specs=tokens,
        check_vma=False,
    )
```

```python
import math

import jax
import jax.numpy as jnp
from jax import lax
from jax.experimental import pallas as pl
from jax.experimental.pallas import tpu as pltpu
from jax.sharding import Mesh
from jax.sharding import PartitionSpec as P

EXPERTS = 2
CAP = 48
PLANE = ("xl", "y", "xh")
VMEM = 20 * 1024 * 1024
GRANT = 30 * 1024 * 1024
LANES = 128
SIDE = 4
TILE = 256
Y_FIRST = 768


def role_of(index):
    return (index // 2) % 2


def selector(ids, rows):
    chosen = [jnp.any(ids == e, axis=1, keepdims=True) for e in range(EXPERTS)]
    flags = jnp.concatenate([c.astype(jnp.float32) for c in chosen], axis=1)
    before = lax.broadcasted_iota(jnp.int32, (rows, rows), 1) < lax.broadcasted_iota(
        jnp.int32, (rows, rows), 0
    )
    rank = jnp.dot(before.astype(jnp.float32), flags, preferred_element_type=jnp.float32)
    slots = lax.broadcasted_iota(jnp.int32, (rows, CAP), 1).astype(jnp.float32)
    return [(rank[:, e : e + 1] == slots) & chosen[e] for e in range(EXPERTS)]


def pick_kernel(ids_ref, logits_ref, tokens_ref, out_ref, place_ref):
    tokens = tokens_ref[...]
    ids = ids_ref[...]
    logits = logits_ref[...]
    top = jnp.max(logits, axis=1, keepdims=True)
    powers = jnp.exp(logits - top)
    probs = (powers / jnp.sum(powers, axis=1, keepdims=True)).astype(jnp.bfloat16)
    probs = probs.astype(jnp.float32)
    marks = selector(ids, tokens.shape[0])
    for e in range(EXPERTS):
        combine = jnp.sum(jnp.where(ids == e, probs, 0.0), axis=1, keepdims=True)
        place_ref[e] = jnp.where(marks[e], combine, 0.0).astype(place_ref.dtype)
        picked = lax.dot_general(
            marks[e].astype(jnp.bfloat16),
            tokens,
            (((0,), (0,)), ((), ())),
            preferred_element_type=jnp.float32,
        ).astype(jnp.bfloat16)
        for k in range(out_ref.shape[0]):
            if role_of(k) == e:
                out_ref[k] = picked


def pick(ids, logits, tokens, chips):
    count, width = tokens.shape
    return pl.pallas_call(
        pick_kernel,
        out_shape=[
            jax.ShapeDtypeStruct((chips, CAP, width), tokens.dtype),
            jax.ShapeDtypeStruct((EXPERTS, count, CAP), tokens.dtype),
        ],
        compiler_params=pltpu.CompilerParams(vmem_limit_bytes=VMEM),
        name="pick_rows",
    )(ids, logits, tokens)


def pack_kernel(at_ref, gate_ref, up_ref, down_ref, first_ref, last_ref, sems):
    rows = first_ref.shape[1]
    start = pl.multiple_of(at_ref[1] * rows, rows)
    spots = (first_ref.at[0], first_ref.at[1], last_ref.at[0])
    copies = [
        pltpu.make_async_copy(ref.at[at_ref[0], pl.ds(start, rows)], spots[n], sems.at[n])
        for n, ref in enumerate((gate_ref, up_ref, down_ref))
    ]
    for copy in copies:
        copy.start()
    for copy in copies:
        copy.wait()


def pack(at, w_gate, w_up, w_down, rows):
    anywhere = pl.BlockSpec(memory_space=pl.ANY)
    return pl.pallas_call(
        pack_kernel,
        out_shape=[
            jax.ShapeDtypeStruct((kinds, rows, w_gate.shape[2]), w_gate.dtype) for kinds in (2, 1)
        ],
        in_specs=[pl.BlockSpec(memory_space=pltpu.SMEM)] + [anywhere] * 3,
        out_specs=[pl.BlockSpec(memory_space=pltpu.VMEM)] * 2,
        scratch_shapes=[pltpu.SemaphoreType.DMA((3,))],
        name="pack_weights",
    )(at, w_gate, w_up, w_down)


def join_kernel(core_ref, own_ref, other_ref, out_ref):
    half = own_ref.shape[2]
    start = pl.multiple_of(core_ref[0] * half, half)
    out_ref[:, :, pl.ds(start, half)] = own_ref[...]
    out_ref[:, :, pl.ds(pl.multiple_of(half - start, half), half)] = other_ref[...]


def join(core, own, other):
    kinds, rows, half = own.shape
    whole = pl.BlockSpec(memory_space=pltpu.VMEM)
    return pl.pallas_call(
        join_kernel,
        in_specs=[pl.BlockSpec(memory_space=pltpu.SMEM), whole, whole],
        out_specs=whole,
        out_shape=jax.ShapeDtypeStruct((kinds, rows, 2 * half), own.dtype),
        compiler_params=pltpu.CompilerParams(vmem_limit_bytes=GRANT),
        name="join_halves",
    )(core, own, other)


def cost(flops, *arrays):
    return pl.CostEstimate(
        flops=flops,
        bytes_accessed=sum(math.prod(a.shape) * jnp.dtype(a.dtype).itemsize for a in arrays),
        transcendentals=0,
    )


def hidden_kernel(*refs):
    x_ref, pieces, (out_ref, held, sems) = refs[0], refs[1:-3], refs[-3:]
    _, share, width = held.shape[1:]
    copies = [
        pltpu.make_async_copy(piece, held.at[k], sems.at[k]) for k, piece in enumerate(pieces)
    ]
    for copy in copies:
        copy.start()
    x = x_ref[...]
    for k, copy in enumerate(copies):
        copy.wait()
        both = lax.dot_general(
            x,
            held[k].reshape(2 * share, width),
            (((1,), (1,)), ((), ())),
            preferred_element_type=jnp.float32,
        )
        gate, up = both[:, :share], both[:, share:]
        out_ref[k, :, :share] = (gate / (1.0 + jnp.exp(-gate)) * up).astype(out_ref.dtype)
        out_ref[k, :, share:] = jnp.zeros((x.shape[0], LANES - share), out_ref.dtype)


def hidden_units(rows, pieces):
    count, width = rows.shape
    shape = pieces[0].shape
    return pl.pallas_call(
        hidden_kernel,
        in_specs=[pl.BlockSpec(memory_space=pltpu.VMEM)]
        + [pl.BlockSpec(memory_space=pl.ANY)] * len(pieces),
        out_specs=pl.BlockSpec(memory_space=pltpu.VMEM),
        out_shape=jax.ShapeDtypeStruct((len(pieces), count, LANES), rows.dtype),
        scratch_shapes=[
            pltpu.VMEM((len(pieces),) + shape, rows.dtype),
            pltpu.SemaphoreType.DMA((len(pieces),)),
        ],
        compiler_params=pltpu.CompilerParams(vmem_limit_bytes=GRANT),
        cost_estimate=cost(4 * count * width * shape[1] * len(pieces), rows, *pieces),
        name="hidden_units",
    )(rows, *pieces)


def down_kernel(spots_ref, hidden_ref, last_ref, *refs):
    weights, out_ref = refs[:-1], refs[-1]
    share, tile = weights[0].shape[1:]
    blank = jnp.zeros((LANES - share, tile), out_ref.dtype)
    hidden = [hidden_ref[k] for k in range(hidden_ref.shape[0])]
    hidden += [last_ref[k] for k in range(last_ref.shape[0])]
    total = None
    for k in range(0, len(weights), 2):
        part = jnp.dot(
            jnp.concatenate(hidden[k : k + 2], axis=1),
            jnp.concatenate([weights[k][0], blank, weights[k + 1][0], blank], axis=0),
            preferred_element_type=jnp.float32,
        )
        total = part if total is None else total + part
    total = total.astype(out_ref.dtype)
    for k in range(SIDE * SIDE):
        out_ref[spots_ref[0, k], spots_ref[1, k]] = total[k * CAP : (k + 1) * CAP]


def down(spots, hidden, last, pieces, first, width, name):
    count = hidden.shape[1]
    share = pieces[0].shape[1]
    out_shape = jax.ShapeDtypeStruct((SIDE, SIDE, CAP, width), hidden.dtype)
    return pl.pallas_call(
        down_kernel,
        grid_spec=pltpu.PrefetchScalarGridSpec(
            num_scalar_prefetch=1,
            grid=(width // TILE,),
            in_specs=[
                pl.BlockSpec(hidden.shape, lambda s, spots: (0, 0, 0)),
                pl.BlockSpec(last.shape, lambda s, spots: (0, 0, 0)),
            ]
            + [pl.BlockSpec((1, share, TILE), lambda s, spots: (0, 0, first // TILE + s))]
            * len(pieces),
            out_specs=pl.BlockSpec((SIDE, SIDE, CAP, TILE), lambda s, spots: (0, 0, 0, s)),
        ),
        out_shape=out_shape,
        compiler_params=pltpu.CompilerParams(vmem_limit_bytes=GRANT),
        cost_estimate=cost(2 * count * width * share * len(pieces), out_shape, out_shape),
        name=name,
    )(spots, hidden, last, *pieces)


def along_z(value, depth):
    pairs = [(z, (z + 1) % depth) for z in range(depth)]
    pairs += [(depth + z, depth + (z - 1) % depth) for z in range(depth)]
    return lax.ppermute(value, ("c", "z"), pairs)


def swapped(value):
    return lax.ppermute(value, "c", [(0, 1), (1, 0)])


def along_x(value, step):
    places = [(x % 2) * 2 + x // 2 for x in range(SIDE)]
    return lax.ppermute(
        value, ("xl", "xh"), [(places[x], places[(x + step) % SIDE]) for x in range(SIDE)]
    )


def along_y(value, step):
    return lax.ppermute(value, "y", [(y, (y + step) % SIDE) for y in range(SIDE)])


def both(first, second):
    return jnp.concatenate([first, second], axis=0)


def body(tokens, expert_ids, route_logits, w_gate, w_up, w_down):
    width = tokens.shape[1]
    chips = lax.axis_size(PLANE)
    depth = lax.axis_size("z")
    share = w_gate.shape[1] // 4
    half = width // 2
    xl, xh, y = lax.axis_index("xl"), lax.axis_index("xh"), lax.axis_index("y")
    core = lax.axis_index("c").astype(jnp.int32)
    at = jnp.stack([y % 2, xl * 2 + y // 2]).astype(jnp.int32)
    sources = jnp.arange(chips, dtype=jnp.int32)
    across = (sources % 2 * 2 + sources // 8 - (xh * 2 + xl)) % SIDE
    along = (sources // 2 % SIDE - y) % SIDE
    x_spots, y_spots = jnp.stack([across, along]), jnp.stack([along, across])

    gate_up, below = pack(at, w_gate, w_up, w_down, share)
    picked, place = pick(expert_ids, route_logits, tokens, chips)
    rows = lax.all_to_all(picked, PLANE, 0, 0).reshape(chips * CAP, width)

    firsts, lasts = [gate_up], [below]
    for _ in range(depth // 2 - 1):
        gate_up, below = along_z(gate_up, depth), along_z(below, depth)
        firsts += [gate_up, swapped(gate_up)]
        lasts += [below, swapped(below)]

    def far(value):
        part = lax.dynamic_slice(value, (0, 0, core * half), value.shape[:2] + (half,))
        return along_z(part, depth)

    gate_up, below = far(gate_up), far(below)
    gate_up, below, rows = lax.optimization_barrier((gate_up, below, rows))
    hidden = hidden_units(rows, firsts)
    lasts.append(join(core.reshape(1), below, swapped(below)))
    last = hidden_units(rows, [join(core.reshape(1), gate_up, swapped(gate_up))])
    first = down(y_spots, hidden, last, lasts, 0, Y_FIRST, "down_y_first")
    first, hidden = lax.optimization_barrier((first, hidden))
    rest = down(x_spots, hidden, last, lasts, Y_FIRST, width - Y_FIRST, "down_x_first")
    return mix(at, place, home_y_first(first), home_x_first(rest))


def home_x_first(terms):
    right, left = along_x(terms[2, :2], 1), along_x(terms[2, 2:], -1)
    right = along_x(both(terms[1, :2] + right, terms[1, 2:]), 1)
    left = along_x(both(terms[3, :2], terms[3, 2:] + left), -1)
    mine = terms[0] + right + left
    return [mine[0], along_y(mine[2], 2), along_y(mine[1], 1), along_y(mine[3], -1)]


def home_y_first(terms):
    over, up, down = along_y(terms[2], 2), along_y(terms[1], 1), along_y(terms[3], -1)
    same, crossed = terms[0] + over, up + down
    pairs = [jnp.stack([same[k], crossed[k]]) for k in range(SIDE)]
    return [pairs[0]] + [along_x(pairs[k], k) for k in range(1, SIDE)]


def both(first, second):
    return jnp.concatenate([first, second], axis=0)


def mix_kernel(at_ref, place_ref, *refs):
    near, far, out_ref = refs[:SIDE], refs[SIDE:-1], refs[-1]
    role = at_ref[0]
    places = [place_ref[role], place_ref[1 - role]]

    def spread(values):
        total = None
        for place, value in zip(places, values):
            high = value.astype(jnp.bfloat16)
            low = (value - high.astype(jnp.float32)).astype(jnp.bfloat16)
            part = jnp.dot(place, high, preferred_element_type=jnp.float32) + jnp.dot(
                place, low, preferred_element_type=jnp.float32
            )
            total = part if total is None else total + part
        return total.astype(out_ref.dtype)

    def wide(value):
        return value.astype(jnp.float32)

    cut = near[0].shape[2]
    out_ref[:, :cut] = spread([sum(wide(ref[e]) for ref in near) for e in range(EXPERTS)])
    out_ref[:, cut:] = spread(
        [wide(far[2 * e][...]) + wide(far[2 * e + 1][...]) for e in range(EXPERTS)]
    )


def mix(at, place, near, far):
    rows = place.shape[1]
    width = near[0].shape[-1] + far[0].shape[-1]
    return pl.pallas_call(
        mix_kernel,
        in_specs=[pl.BlockSpec(memory_space=pltpu.SMEM)]
        + [pl.BlockSpec(memory_space=pltpu.VMEM)] * (1 + len(near) + len(far)),
        out_specs=pl.BlockSpec(memory_space=pltpu.VMEM),
        out_shape=jax.ShapeDtypeStruct((rows, width), jnp.bfloat16),
        compiler_params=pltpu.CompilerParams(vmem_limit_bytes=GRANT),
        name="mix_terms",
    )(at, place, *near, *far)


def solution(mesh):
    fine = Mesh(mesh.devices.reshape(2, 4, 2, 8, 2), ("xl", "y", "c", "z", "xh"))
    tokens = P(("xl", "y", "c", "z", "xh"), None)
    weights = P(None, ("z", "xh"), None)
    return jax.shard_map(
        body,
        mesh=fine,
        in_specs=(tokens,) * 3 + (weights,) * 3,
        out_specs=tokens,
        check_vma=False,
    )
```

```python
import math

import jax
import jax.numpy as jnp
from jax import lax
from jax.experimental import pallas as pl
from jax.experimental.pallas import tpu as pltpu
from jax.sharding import Mesh
from jax.sharding import PartitionSpec as P

EXPERTS = 2
CAP = 48
PLANE = ("xl", "y", "xh")
VMEM = 20 * 1024 * 1024
GRANT = 30 * 1024 * 1024
LANES = 128
SIDE = 4
TILE = 256
Y_FIRST = 768
EARLY = 5


def role_of(index):
    return (index // 2) % 2


def selector(ids, rows):
    chosen = [jnp.any(ids == e, axis=1, keepdims=True) for e in range(EXPERTS)]
    flags = jnp.concatenate([c.astype(jnp.float32) for c in chosen], axis=1)
    before = lax.broadcasted_iota(jnp.int32, (rows, rows), 1) < lax.broadcasted_iota(
        jnp.int32, (rows, rows), 0
    )
    rank = jnp.dot(before.astype(jnp.float32), flags, preferred_element_type=jnp.float32)
    slots = lax.broadcasted_iota(jnp.int32, (rows, CAP), 1).astype(jnp.float32)
    return [(rank[:, e : e + 1] == slots) & chosen[e] for e in range(EXPERTS)]


def pick_kernel(ids_ref, logits_ref, tokens_ref, out_ref, place_ref):
    tokens = tokens_ref[...]
    ids = ids_ref[...]
    logits = logits_ref[...]
    top = jnp.max(logits, axis=1, keepdims=True)
    powers = jnp.exp(logits - top)
    probs = (powers / jnp.sum(powers, axis=1, keepdims=True)).astype(jnp.bfloat16)
    probs = probs.astype(jnp.float32)
    marks = selector(ids, tokens.shape[0])
    for e in range(EXPERTS):
        combine = jnp.sum(jnp.where(ids == e, probs, 0.0), axis=1, keepdims=True)
        place_ref[e] = jnp.where(marks[e], combine, 0.0).astype(place_ref.dtype)
        picked = lax.dot_general(
            marks[e].astype(jnp.bfloat16),
            tokens,
            (((0,), (0,)), ((), ())),
            preferred_element_type=jnp.float32,
        ).astype(jnp.bfloat16)
        for k in range(out_ref.shape[0]):
            if role_of(k) == e:
                out_ref[k] = picked


def pick(ids, logits, tokens, chips):
    count, width = tokens.shape
    return pl.pallas_call(
        pick_kernel,
        out_shape=[
            jax.ShapeDtypeStruct((chips, CAP, width), tokens.dtype),
            jax.ShapeDtypeStruct((EXPERTS, count, CAP), tokens.dtype),
        ],
        compiler_params=pltpu.CompilerParams(vmem_limit_bytes=VMEM),
        name="pick_rows",
    )(ids, logits, tokens)


def pack_kernel(at_ref, gate_ref, up_ref, down_ref, first_ref, last_ref, sems):
    rows = first_ref.shape[1]
    start = pl.multiple_of(at_ref[1] * rows, rows)
    spots = (first_ref.at[0], first_ref.at[1], last_ref.at[0])
    copies = [
        pltpu.make_async_copy(ref.at[at_ref[0], pl.ds(start, rows)], spots[n], sems.at[n])
        for n, ref in enumerate((gate_ref, up_ref, down_ref))
    ]
    for copy in copies:
        copy.start()
    for copy in copies:
        copy.wait()


def pack(at, w_gate, w_up, w_down, rows):
    anywhere = pl.BlockSpec(memory_space=pl.ANY)
    return pl.pallas_call(
        pack_kernel,
        out_shape=[
            jax.ShapeDtypeStruct((kinds, rows, w_gate.shape[2]), w_gate.dtype) for kinds in (2, 1)
        ],
        in_specs=[pl.BlockSpec(memory_space=pltpu.SMEM)] + [anywhere] * 3,
        out_specs=[pl.BlockSpec(memory_space=pltpu.VMEM)] * 2,
        scratch_shapes=[pltpu.SemaphoreType.DMA((3,))],
        name="pack_weights",
    )(at, w_gate, w_up, w_down)


def cost(flops, *arrays):
    return pl.CostEstimate(
        flops=flops,
        bytes_accessed=sum(math.prod(a.shape) * jnp.dtype(a.dtype).itemsize for a in arrays),
        transcendentals=0,
    )


def activate(x, weights, share):
    both = None
    for columns, part in weights:
        product = lax.dot_general(
            x[:, columns], part, (((1,), (1,)), ((), ())), preferred_element_type=jnp.float32
        )
        both = product if both is None else both + product
    gate, up = both[:, :share], both[:, share:]
    return (gate / (1.0 + jnp.exp(-gate)) * up).astype(jnp.bfloat16)


def hidden_kernel(x_ref, *refs):
    pieces, out_ref = refs[:-1], refs[-1]
    _, share, width = pieces[0].shape
    blank = jnp.zeros((x_ref.shape[0], LANES - share), out_ref.dtype)
    for k, piece in enumerate(pieces):
        weights = piece[...].reshape(2 * share, width)
        units = activate(x_ref, [(slice(None), weights)], share)
        out_ref[:, k * LANES : k * LANES + share] = units
        out_ref[:, k * LANES + share : (k + 1) * LANES] = blank


def hidden_units(rows, pieces):
    count, width = rows.shape
    share = pieces[0].shape[1]
    whole = pl.BlockSpec(memory_space=pltpu.VMEM)
    return pl.pallas_call(
        hidden_kernel,
        in_specs=[whole] * (1 + len(pieces)),
        out_specs=whole,
        out_shape=jax.ShapeDtypeStruct((count, len(pieces) * LANES), rows.dtype),
        compiler_params=pltpu.CompilerParams(vmem_limit_bytes=GRANT),
        cost_estimate=cost(4 * count * width * share * len(pieces), rows, *pieces),
        name="hidden_units",
    )(rows, *pieces)


def finish_kernel(core_ref, spots_ref, x_ref, early_ref, late_ref, own_ref, other_ref, *refs):
    weights, (below_own, below_other, first_ref, rest_ref, held, sems) = refs[:-6], refs[-6:]
    pieces, share, width = held.shape
    half = width // 2
    near = pl.ds(pl.multiple_of(core_ref[0] * half, half), half)
    distant = pl.ds(pl.multiple_of(half - core_ref[0] * half, half), half)
    copies = [
        pltpu.make_async_copy(ref.at[0], held.at[k], sems.at[k]) for k, ref in enumerate(weights)
    ]
    last = pieces - 1
    copies += [
        pltpu.make_async_copy(below_own.at[0], held.at[last, :, near], sems.at[last]),
        pltpu.make_async_copy(below_other.at[0], held.at[last, :, distant], sems.at[last + 1]),
    ]
    for copy in copies:
        copy.start()
    units = activate(
        x_ref,
        [
            (near, own_ref[...].reshape(2 * share, half)),
            (distant, other_ref[...].reshape(2 * share, half)),
        ],
        share,
    )
    blank = jnp.zeros((units.shape[0], LANES - share), units.dtype)
    hidden = jnp.concatenate([early_ref[...], late_ref[...], units, blank], axis=1)
    for copy in copies:
        copy.wait()
    gap = jnp.zeros((LANES - share, TILE), units.dtype)
    cut = first_ref.shape[3]
    for start in range(0, width, TILE):
        parts = []
        for k in range(pieces):
            parts += [held[k, :, start : start + TILE], gap]
        total = jnp.dot(
            hidden, jnp.concatenate(parts, axis=0), preferred_element_type=jnp.float32
        ).astype(units.dtype)
        for k in range(SIDE * SIDE):
            value = total[k * CAP : (k + 1) * CAP]
            across, along = spots_ref[0, k], spots_ref[1, k]
            if start < cut:
                first_ref[along, across, :, start : start + TILE] = value
            else:
                rest_ref[across, along, :, start - cut : start - cut + TILE] = value


def finish(core, spots, rows, early, late, halves, pieces, below):
    count, width = rows.shape
    share = pieces[0].shape[1]
    whole = pl.BlockSpec(memory_space=pltpu.VMEM)
    scalars = pl.BlockSpec(memory_space=pltpu.SMEM)
    anywhere = pl.BlockSpec(memory_space=pltpu.HBM)
    number = len(pieces) + 1
    return pl.pallas_call(
        finish_kernel,
        in_specs=[scalars] * 2 + [whole] * 5 + [anywhere] * (number + 1),
        out_specs=[whole] * 2,
        out_shape=[
            jax.ShapeDtypeStruct((SIDE, SIDE, CAP, columns), rows.dtype)
            for columns in (Y_FIRST, width - Y_FIRST)
        ],
        scratch_shapes=[
            pltpu.VMEM((number, share, width), rows.dtype),
            pltpu.SemaphoreType.DMA((number + 1,)),
        ],
        compiler_params=pltpu.CompilerParams(vmem_limit_bytes=GRANT),
        cost_estimate=cost(2 * count * width * share * (number + 2), rows, rows, *pieces),
        name="finish_terms",
    )(core, spots, rows, early, late, *halves, *pieces, *below)


def along_z(value, depth):
    pairs = [(z, (z + 1) % depth) for z in range(depth)]
    pairs += [(depth + z, depth + (z - 1) % depth) for z in range(depth)]
    return lax.ppermute(value, ("c", "z"), pairs)


def swapped(value):
    return lax.ppermute(value, "c", [(0, 1), (1, 0)])


def along_x(value, step):
    places = [(x % 2) * 2 + x // 2 for x in range(SIDE)]
    return lax.ppermute(
        value, ("xl", "xh"), [(places[x], places[(x + step) % SIDE]) for x in range(SIDE)]
    )


def along_y(value, step):
    return lax.ppermute(value, "y", [(y, (y + step) % SIDE) for y in range(SIDE)])


def both(first, second):
    return jnp.concatenate([first, second], axis=0)


def body(tokens, expert_ids, route_logits, w_gate, w_up, w_down):
    width = tokens.shape[1]
    chips = lax.axis_size(PLANE)
    depth = lax.axis_size("z")
    share = w_gate.shape[1] // 4
    half = width // 2
    xl, xh, y = lax.axis_index("xl"), lax.axis_index("xh"), lax.axis_index("y")
    core = lax.axis_index("c").astype(jnp.int32)
    at = jnp.stack([y % 2, xl * 2 + y // 2]).astype(jnp.int32)
    sources = jnp.arange(chips, dtype=jnp.int32)
    across = (sources % 2 * 2 + sources // 8 - (xh * 2 + xl)) % SIDE
    along = (sources // 2 % SIDE - y) % SIDE
    spots = jnp.stack([across, along])

    gate_up, below = pack(at, w_gate, w_up, w_down, share)
    picked, place = pick(expert_ids, route_logits, tokens, chips)
    rows = lax.all_to_all(picked, PLANE, 0, 0).reshape(chips * CAP, width)

    firsts, lasts = [gate_up], [below]
    for _ in range(depth // 2 - 1):
        gate_up, below = along_z(gate_up, depth), along_z(below, depth)
        gate_up, below = lax.optimization_barrier((gate_up, below))
        firsts += [gate_up, swapped(gate_up)]
        lasts += [below, swapped(below)]

    def far(value):
        part = lax.dynamic_slice(value, (0, 0, core * half), value.shape[:2] + (half,))
        return along_z(part, depth)

    gate_up, below = far(gate_up), far(below)
    early = hidden_units(rows, firsts[:EARLY])
    late = hidden_units(rows, firsts[EARLY:])
    gate_up, below, early = lax.optimization_barrier((gate_up, below, early))
    first, rest = finish(
        core.reshape(1),
        spots,
        rows,
        early,
        late,
        (gate_up, swapped(gate_up)),
        lasts,
        (below, swapped(below)),
    )
    return mix(at, place, home_y_first(first), home_x_first(rest))


def home_x_first(terms):
    right, left = along_x(terms[2, :2], 1), along_x(terms[2, 2:], -1)
    right = along_x(both(terms[1, :2] + right, terms[1, 2:]), 1)
    left = along_x(both(terms[3, :2], terms[3, 2:] + left), -1)
    mine = terms[0] + right + left
    return [mine[0], along_y(mine[2], 2), along_y(mine[1], 1), along_y(mine[3], -1)]


def home_y_first(terms):
    over, up, down = along_y(terms[2], 2), along_y(terms[1], 1), along_y(terms[3], -1)
    same, crossed = terms[0] + over, up + down
    pairs = [jnp.stack([same[k], crossed[k]]) for k in range(SIDE)]
    return [pairs[0]] + [along_x(pairs[k], k) for k in range(1, SIDE)]


def both(first, second):
    return jnp.concatenate([first, second], axis=0)


def mix_kernel(at_ref, place_ref, *refs):
    near, far, out_ref = refs[:SIDE], refs[SIDE:-1], refs[-1]
    role = at_ref[0]
    places = [place_ref[role], place_ref[1 - role]]

    def spread(values):
        total = None
        for place, value in zip(places, values):
            high = value.astype(jnp.bfloat16)
            low = (value - high.astype(jnp.float32)).astype(jnp.bfloat16)
            part = jnp.dot(place, high, preferred_element_type=jnp.float32) + jnp.dot(
                place, low, preferred_element_type=jnp.float32
            )
            total = part if total is None else total + part
        return total.astype(out_ref.dtype)

    def wide(value):
        return value.astype(jnp.float32)

    cut = near[0].shape[2]
    out_ref[:, :cut] = spread([sum(wide(ref[e]) for ref in near) for e in range(EXPERTS)])
    out_ref[:, cut:] = spread(
        [wide(far[2 * e][...]) + wide(far[2 * e + 1][...]) for e in range(EXPERTS)]
    )


def mix(at, place, near, far):
    rows = place.shape[1]
    width = near[0].shape[-1] + far[0].shape[-1]
    return pl.pallas_call(
        mix_kernel,
        in_specs=[pl.BlockSpec(memory_space=pltpu.SMEM)]
        + [pl.BlockSpec(memory_space=pltpu.VMEM)] * (1 + len(near) + len(far)),
        out_specs=pl.BlockSpec(memory_space=pltpu.VMEM),
        out_shape=jax.ShapeDtypeStruct((rows, width), jnp.bfloat16),
        compiler_params=pltpu.CompilerParams(vmem_limit_bytes=GRANT),
        name="mix_terms",
    )(at, place, *near, *far)


def solution(mesh):
    fine = Mesh(mesh.devices.reshape(2, 4, 2, 8, 2), ("xl", "y", "c", "z", "xh"))
    tokens = P(("xl", "y", "c", "z", "xh"), None)
    weights = P(None, ("z", "xh"), None)
    return jax.shard_map(
        body,
        mesh=fine,
        in_specs=(tokens,) * 3 + (weights,) * 3,
        out_specs=tokens,
        check_vma=False,
    )
```

```python
import math

import jax
import jax.numpy as jnp
from jax import lax
from jax.experimental import pallas as pl
from jax.experimental.pallas import tpu as pltpu
from jax.sharding import Mesh
from jax.sharding import PartitionSpec as P

EXPERTS = 2
CAP = 48
PLANE = ("xl", "y", "xh")
VMEM = 20 * 1024 * 1024
GRANT = 30 * 1024 * 1024
LANES = 128
SIDE = 4
TILE = 256
Y_FIRST = 768
EARLY = 5


def role_of(index):
    return (index // 2) % 2


def selector(ids, rows):
    chosen = [jnp.any(ids == e, axis=1, keepdims=True) for e in range(EXPERTS)]
    flags = jnp.concatenate([c.astype(jnp.float32) for c in chosen], axis=1)
    before = lax.broadcasted_iota(jnp.int32, (rows, rows), 1) < lax.broadcasted_iota(
        jnp.int32, (rows, rows), 0
    )
    rank = jnp.dot(before.astype(jnp.float32), flags, preferred_element_type=jnp.float32)
    slots = lax.broadcasted_iota(jnp.int32, (rows, CAP), 1).astype(jnp.float32)
    return [(rank[:, e : e + 1] == slots) & chosen[e] for e in range(EXPERTS)]


def pick_kernel(ids_ref, logits_ref, tokens_ref, out_ref, place_ref):
    tokens = tokens_ref[...]
    ids = ids_ref[...]
    logits = logits_ref[...]
    top = jnp.max(logits, axis=1, keepdims=True)
    powers = jnp.exp(logits - top)
    probs = (powers / jnp.sum(powers, axis=1, keepdims=True)).astype(jnp.bfloat16)
    probs = probs.astype(jnp.float32)
    marks = selector(ids, tokens.shape[0])
    for e in range(EXPERTS):
        combine = jnp.sum(jnp.where(ids == e, probs, 0.0), axis=1, keepdims=True)
        place_ref[e] = jnp.where(marks[e], combine, 0.0).astype(place_ref.dtype)
        picked = lax.dot_general(
            marks[e].astype(jnp.bfloat16),
            tokens,
            (((0,), (0,)), ((), ())),
            preferred_element_type=jnp.float32,
        ).astype(jnp.bfloat16)
        for k in range(out_ref.shape[0]):
            if role_of(k) == e:
                out_ref[k] = picked


def pick(ids, logits, tokens, chips):
    count, width = tokens.shape
    return pl.pallas_call(
        pick_kernel,
        out_shape=[
            jax.ShapeDtypeStruct((chips, CAP, width), tokens.dtype),
            jax.ShapeDtypeStruct((EXPERTS, count, CAP), tokens.dtype),
        ],
        compiler_params=pltpu.CompilerParams(vmem_limit_bytes=VMEM),
        name="pick_rows",
    )(ids, logits, tokens)


def pack_kernel(at_ref, gate_ref, up_ref, down_ref, first_ref, last_ref, sems):
    rows = first_ref.shape[1]
    start = pl.multiple_of(at_ref[1] * rows, rows)
    spots = (first_ref.at[0], first_ref.at[1], last_ref.at[0])
    copies = [
        pltpu.make_async_copy(ref.at[at_ref[0], pl.ds(start, rows)], spots[n], sems.at[n])
        for n, ref in enumerate((gate_ref, up_ref, down_ref))
    ]
    for copy in copies:
        copy.start()
    for copy in copies:
        copy.wait()


def pack(at, w_gate, w_up, w_down, rows):
    anywhere = pl.BlockSpec(memory_space=pl.ANY)
    return pl.pallas_call(
        pack_kernel,
        out_shape=[
            jax.ShapeDtypeStruct((kinds, rows, w_gate.shape[2]), w_gate.dtype) for kinds in (2, 1)
        ],
        in_specs=[pl.BlockSpec(memory_space=pltpu.SMEM)] + [anywhere] * 3,
        out_specs=[pl.BlockSpec(memory_space=pltpu.VMEM)] * 2,
        scratch_shapes=[pltpu.SemaphoreType.DMA((3,))],
        name="pack_weights",
    )(at, w_gate, w_up, w_down)


def halve_kernel(core_ref, *refs):
    number = len(refs) // 2
    for source, target in zip(refs[:number], refs[number:]):
        half = target.shape[2]
        target[...] = source[:, :, pl.ds(pl.multiple_of(core_ref[0] * half, half), half)]


def halve(core, *arrays):
    whole = pl.BlockSpec(memory_space=pltpu.VMEM)
    return pl.pallas_call(
        halve_kernel,
        in_specs=[pl.BlockSpec(memory_space=pltpu.SMEM)] + [whole] * len(arrays),
        out_specs=[whole] * len(arrays),
        out_shape=[
            jax.ShapeDtypeStruct(a.shape[:2] + (a.shape[2] // 2,), a.dtype) for a in arrays
        ],
        compiler_params=pltpu.CompilerParams(vmem_limit_bytes=GRANT),
        name="halve_pieces",
    )(core, *arrays)


def cost(flops, *arrays):
    return pl.CostEstimate(
        flops=flops,
        bytes_accessed=sum(math.prod(a.shape) * jnp.dtype(a.dtype).itemsize for a in arrays),
        transcendentals=0,
    )


def activate(x, weights, share):
    both = None
    for columns, part in weights:
        product = lax.dot_general(
            x[:, columns], part, (((1,), (1,)), ((), ())), preferred_element_type=jnp.float32
        )
        both = product if both is None else both + product
    gate, up = both[:, :share], both[:, share:]
    return (gate / (1.0 + jnp.exp(-gate)) * up).astype(jnp.bfloat16)


def hidden_kernel(x_ref, *refs):
    pieces, out_ref = refs[:-1], refs[-1]
    _, share, width = pieces[0].shape
    blank = jnp.zeros((x_ref.shape[0], LANES - share), out_ref.dtype)
    for k, piece in enumerate(pieces):
        weights = piece[...].reshape(2 * share, width)
        units = activate(x_ref, [(slice(None), weights)], share)
        out_ref[:, k * LANES : k * LANES + share] = units
        out_ref[:, k * LANES + share : (k + 1) * LANES] = blank


def hidden_units(rows, pieces):
    count, width = rows.shape
    share = pieces[0].shape[1]
    whole = pl.BlockSpec(memory_space=pltpu.VMEM)
    return pl.pallas_call(
        hidden_kernel,
        in_specs=[whole] * (1 + len(pieces)),
        out_specs=whole,
        out_shape=jax.ShapeDtypeStruct((count, len(pieces) * LANES), rows.dtype),
        compiler_params=pltpu.CompilerParams(vmem_limit_bytes=GRANT),
        cost_estimate=cost(4 * count * width * share * len(pieces), rows, *pieces),
        name="hidden_units",
    )(rows, *pieces)


def finish_kernel(core_ref, spots_ref, x_ref, early_ref, late_ref, own_ref, other_ref, *refs):
    weights, (below_own, below_other, first_ref, rest_ref, held, sems) = refs[:-6], refs[-6:]
    pieces, share, width = held.shape
    half = width // 2
    near = pl.ds(pl.multiple_of(core_ref[0] * half, half), half)
    distant = pl.ds(pl.multiple_of(half - core_ref[0] * half, half), half)
    copies = [
        pltpu.make_async_copy(ref.at[0], held.at[k], sems.at[k]) for k, ref in enumerate(weights)
    ]
    last = pieces - 1
    copies += [
        pltpu.make_async_copy(below_own.at[0], held.at[last, :, near], sems.at[last]),
        pltpu.make_async_copy(below_other.at[0], held.at[last, :, distant], sems.at[last + 1]),
    ]
    for copy in copies:
        copy.start()
    units = activate(
        x_ref,
        [
            (near, own_ref[...].reshape(2 * share, half)),
            (distant, other_ref[...].reshape(2 * share, half)),
        ],
        share,
    )
    blank = jnp.zeros((units.shape[0], LANES - share), units.dtype)
    hidden = jnp.concatenate([early_ref[...], late_ref[...], units, blank], axis=1)
    for copy in copies:
        copy.wait()
    gap = jnp.zeros((LANES - share, TILE), units.dtype)
    cut = first_ref.shape[3]
    for start in range(0, width, TILE):
        parts = []
        for k in range(pieces):
            parts += [held[k, :, start : start + TILE], gap]
        total = jnp.dot(
            hidden, jnp.concatenate(parts, axis=0), preferred_element_type=jnp.float32
        ).astype(units.dtype)
        for k in range(SIDE * SIDE):
            value = total[k * CAP : (k + 1) * CAP]
            across, along = spots_ref[0, k], spots_ref[1, k]
            if start < cut:
                first_ref[along, across, :, start : start + TILE] = value
            else:
                rest_ref[across, along, :, start - cut : start - cut + TILE] = value


def finish(core, spots, rows, early, late, halves, pieces, below):
    count, width = rows.shape
    share = pieces[0].shape[1]
    whole = pl.BlockSpec(memory_space=pltpu.VMEM)
    scalars = pl.BlockSpec(memory_space=pltpu.SMEM)
    anywhere = pl.BlockSpec(memory_space=pltpu.HBM)
    number = len(pieces) + 1
    return pl.pallas_call(
        finish_kernel,
        in_specs=[scalars] * 2 + [whole] * 5 + [anywhere] * (number + 1),
        out_specs=[whole] * 2,
        out_shape=[
            jax.ShapeDtypeStruct((SIDE, SIDE, CAP, columns), rows.dtype)
            for columns in (Y_FIRST, width - Y_FIRST)
        ],
        scratch_shapes=[
            pltpu.VMEM((number, share, width), rows.dtype),
            pltpu.SemaphoreType.DMA((number + 1,)),
        ],
        compiler_params=pltpu.CompilerParams(vmem_limit_bytes=GRANT),
        cost_estimate=cost(2 * count * width * share * (number + 2), rows, rows, *pieces),
        name="finish_terms",
    )(core, spots, rows, early, late, *halves, *pieces, *below)


def along_z(value, depth):
    pairs = [(z, (z + 1) % depth) for z in range(depth)]
    pairs += [(depth + z, depth + (z - 1) % depth) for z in range(depth)]
    return lax.ppermute(value, ("c", "z"), pairs)


def swapped(value):
    return lax.ppermute(value, "c", [(0, 1), (1, 0)])


def along_x(value, step):
    places = [(x % 2) * 2 + x // 2 for x in range(SIDE)]
    return lax.ppermute(
        value, ("xl", "xh"), [(places[x], places[(x + step) % SIDE]) for x in range(SIDE)]
    )


def along_y(value, step):
    return lax.ppermute(value, "y", [(y, (y + step) % SIDE) for y in range(SIDE)])


def both(first, second):
    return jnp.concatenate([first, second], axis=0)


def body(tokens, expert_ids, route_logits, w_gate, w_up, w_down):
    width = tokens.shape[1]
    chips = lax.axis_size(PLANE)
    depth = lax.axis_size("z")
    share = w_gate.shape[1] // 4
    xl, xh, y = lax.axis_index("xl"), lax.axis_index("xh"), lax.axis_index("y")
    core = lax.axis_index("c").astype(jnp.int32)
    at = jnp.stack([y % 2, xl * 2 + y // 2]).astype(jnp.int32)
    sources = jnp.arange(chips, dtype=jnp.int32)
    across = (sources % 2 * 2 + sources // 8 - (xh * 2 + xl)) % SIDE
    along = (sources // 2 % SIDE - y) % SIDE
    spots = jnp.stack([across, along])

    gate_up, below = pack(at, w_gate, w_up, w_down, share)
    picked, place = pick(expert_ids, route_logits, tokens, chips)
    rows = lax.all_to_all(picked, PLANE, 0, 0).reshape(chips * CAP, width)

    firsts, lasts = [gate_up], [below]
    for _ in range(depth // 2 - 1):
        gate_up, below = along_z(gate_up, depth), along_z(below, depth)
        gate_up, below = lax.optimization_barrier((gate_up, below))
        firsts += [gate_up, swapped(gate_up)]
        lasts += [below, swapped(below)]

    gate_up, below = halve(core.reshape(1), gate_up, below)
    gate_up, below = along_z(gate_up, depth), along_z(below, depth)
    early = hidden_units(rows, firsts[:EARLY])
    late = hidden_units(rows, firsts[EARLY:])
    gate_up, below, early = lax.optimization_barrier((gate_up, below, early))
    first, rest = finish(
        core.reshape(1),
        spots,
        rows,
        early,
        late,
        (gate_up, swapped(gate_up)),
        lasts,
        (below, swapped(below)),
    )
    return mix(at, place, home_y_first(first), home_x_first(rest))


def home_x_first(terms):
    right, left = along_x(terms[2, :2], 1), along_x(terms[2, 2:], -1)
    right = along_x(both(terms[1, :2] + right, terms[1, 2:]), 1)
    left = along_x(both(terms[3, :2], terms[3, 2:] + left), -1)
    mine = terms[0] + right + left
    return [mine[0], along_y(mine[2], 2), along_y(mine[1], 1), along_y(mine[3], -1)]


def home_y_first(terms):
    over, up, down = along_y(terms[2], 2), along_y(terms[1], 1), along_y(terms[3], -1)
    same, crossed = terms[0] + over, up + down
    pairs = [jnp.stack([same[k], crossed[k]]) for k in range(SIDE)]
    return [pairs[0]] + [along_x(pairs[k], k) for k in range(1, SIDE)]


def both(first, second):
    return jnp.concatenate([first, second], axis=0)


def mix_kernel(at_ref, place_ref, *refs):
    near, far, out_ref = refs[:SIDE], refs[SIDE:-1], refs[-1]
    role = at_ref[0]
    places = [place_ref[role], place_ref[1 - role]]

    def spread(values):
        total = None
        for place, value in zip(places, values):
            high = value.astype(jnp.bfloat16)
            low = (value - high.astype(jnp.float32)).astype(jnp.bfloat16)
            part = jnp.dot(place, high, preferred_element_type=jnp.float32) + jnp.dot(
                place, low, preferred_element_type=jnp.float32
            )
            total = part if total is None else total + part
        return total.astype(out_ref.dtype)

    def wide(value):
        return value.astype(jnp.float32)

    cut = near[0].shape[2]
    out_ref[:, :cut] = spread([sum(wide(ref[e]) for ref in near) for e in range(EXPERTS)])
    out_ref[:, cut:] = spread(
        [wide(far[2 * e][...]) + wide(far[2 * e + 1][...]) for e in range(EXPERTS)]
    )


def mix(at, place, near, far):
    rows = place.shape[1]
    width = near[0].shape[-1] + far[0].shape[-1]
    return pl.pallas_call(
        mix_kernel,
        in_specs=[pl.BlockSpec(memory_space=pltpu.SMEM)]
        + [pl.BlockSpec(memory_space=pltpu.VMEM)] * (1 + len(near) + len(far)),
        out_specs=pl.BlockSpec(memory_space=pltpu.VMEM),
        out_shape=jax.ShapeDtypeStruct((rows, width), jnp.bfloat16),
        compiler_params=pltpu.CompilerParams(vmem_limit_bytes=GRANT),
        name="mix_terms",
    )(at, place, *near, *far)


def solution(mesh):
    fine = Mesh(mesh.devices.reshape(2, 4, 2, 8, 2), ("xl", "y", "c", "z", "xh"))
    tokens = P(("xl", "y", "c", "z", "xh"), None)
    weights = P(None, ("z", "xh"), None)
    return jax.shard_map(
        body,
        mesh=fine,
        in_specs=(tokens,) * 3 + (weights,) * 3,
        out_specs=tokens,
        check_vma=False,
    )
```

```python
import math

import jax
import jax.numpy as jnp
from jax import lax
from jax.experimental import pallas as pl
from jax.experimental.pallas import tpu as pltpu
from jax.sharding import Mesh
from jax.sharding import PartitionSpec as P

EXPERTS = 2
CAP = 48
PLANE = ("xl", "y", "xh")
VMEM = 20 * 1024 * 1024
GRANT = 18 * 1024 * 1024
LANES = 128
SIDE = 4
TILE = 256
Y_FIRST = 768
EARLY = 5


def role_of(index):
    return (index // 2) % 2


def selector(ids, rows):
    chosen = [jnp.any(ids == e, axis=1, keepdims=True) for e in range(EXPERTS)]
    flags = jnp.concatenate([c.astype(jnp.float32) for c in chosen], axis=1)
    before = lax.broadcasted_iota(jnp.int32, (rows, rows), 1) < lax.broadcasted_iota(
        jnp.int32, (rows, rows), 0
    )
    rank = jnp.dot(before.astype(jnp.float32), flags, preferred_element_type=jnp.float32)
    slots = lax.broadcasted_iota(jnp.int32, (rows, CAP), 1).astype(jnp.float32)
    return [(rank[:, e : e + 1] == slots) & chosen[e] for e in range(EXPERTS)]


def pick_kernel(ids_ref, logits_ref, tokens_ref, out_ref, place_ref):
    tokens = tokens_ref[...]
    ids = ids_ref[...]
    logits = logits_ref[...]
    top = jnp.max(logits, axis=1, keepdims=True)
    powers = jnp.exp(logits - top)
    probs = (powers / jnp.sum(powers, axis=1, keepdims=True)).astype(jnp.bfloat16)
    probs = probs.astype(jnp.float32)
    marks = selector(ids, tokens.shape[0])
    for e in range(EXPERTS):
        combine = jnp.sum(jnp.where(ids == e, probs, 0.0), axis=1, keepdims=True)
        place_ref[e] = jnp.where(marks[e], combine, 0.0).astype(place_ref.dtype)
        picked = lax.dot_general(
            marks[e].astype(jnp.bfloat16),
            tokens,
            (((0,), (0,)), ((), ())),
            preferred_element_type=jnp.float32,
        ).astype(jnp.bfloat16)
        for k in range(out_ref.shape[0]):
            if role_of(k) == e:
                out_ref[k] = picked


def pick(ids, logits, tokens, chips):
    count, width = tokens.shape
    return pl.pallas_call(
        pick_kernel,
        out_shape=[
            jax.ShapeDtypeStruct((chips, CAP, width), tokens.dtype),
            jax.ShapeDtypeStruct((EXPERTS, count, CAP), tokens.dtype),
        ],
        compiler_params=pltpu.CompilerParams(vmem_limit_bytes=VMEM),
        name="pick_rows",
    )(ids, logits, tokens)


def pack_kernel(at_ref, gate_ref, up_ref, down_ref, first_ref, last_ref, sems):
    rows = first_ref.shape[1]
    start = pl.multiple_of(at_ref[1] * rows, rows)
    spots = (first_ref.at[0], first_ref.at[1], last_ref.at[0])
    copies = [
        pltpu.make_async_copy(ref.at[at_ref[0], pl.ds(start, rows)], spots[n], sems.at[n])
        for n, ref in enumerate((gate_ref, up_ref, down_ref))
    ]
    for copy in copies:
        copy.start()
    for copy in copies:
        copy.wait()


def pack(at, w_gate, w_up, w_down, rows):
    anywhere = pl.BlockSpec(memory_space=pl.ANY)
    return pl.pallas_call(
        pack_kernel,
        out_shape=[
            jax.ShapeDtypeStruct((kinds, rows, w_gate.shape[2]), w_gate.dtype) for kinds in (2, 1)
        ],
        in_specs=[pl.BlockSpec(memory_space=pltpu.SMEM)] + [anywhere] * 3,
        out_specs=[pl.BlockSpec(memory_space=pltpu.VMEM)] * 2,
        scratch_shapes=[pltpu.SemaphoreType.DMA((3,))],
        name="pack_weights",
    )(at, w_gate, w_up, w_down)


def halve_kernel(core_ref, *refs):
    number = len(refs) // 2
    for source, target in zip(refs[:number], refs[number:]):
        half = target.shape[2]
        target[...] = source[:, :, pl.ds(pl.multiple_of(core_ref[0] * half, half), half)]


def halve(core, *arrays):
    whole = pl.BlockSpec(memory_space=pltpu.VMEM)
    return pl.pallas_call(
        halve_kernel,
        in_specs=[pl.BlockSpec(memory_space=pltpu.SMEM)] + [whole] * len(arrays),
        out_specs=[whole] * len(arrays),
        out_shape=[
            jax.ShapeDtypeStruct(a.shape[:2] + (a.shape[2] // 2,), a.dtype) for a in arrays
        ],
        compiler_params=pltpu.CompilerParams(vmem_limit_bytes=GRANT),
        name="halve_pieces",
    )(core, *arrays)


def cost(flops, *arrays):
    return pl.CostEstimate(
        flops=flops,
        bytes_accessed=sum(math.prod(a.shape) * jnp.dtype(a.dtype).itemsize for a in arrays),
        transcendentals=0,
    )


def activate(x, weights, share):
    both = None
    for columns, part in weights:
        product = lax.dot_general(
            x[:, columns], part, (((1,), (1,)), ((), ())), preferred_element_type=jnp.float32
        )
        both = product if both is None else both + product
    gate, up = both[:, :share], both[:, share:]
    return (gate / (1.0 + jnp.exp(-gate)) * up).astype(jnp.bfloat16)


def hidden_kernel(x_ref, *refs):
    pieces, out_ref = refs[:-1], refs[-1]
    _, share, width = pieces[0].shape
    blank = jnp.zeros((x_ref.shape[0], LANES - share), out_ref.dtype)
    for k, piece in enumerate(pieces):
        weights = piece[...].reshape(2 * share, width)
        units = activate(x_ref, [(slice(None), weights)], share)
        out_ref[:, k * LANES : k * LANES + share] = units
        out_ref[:, k * LANES + share : (k + 1) * LANES] = blank


def hidden_units(rows, pieces):
    count, width = rows.shape
    share = pieces[0].shape[1]
    whole = pl.BlockSpec(memory_space=pltpu.VMEM)
    return pl.pallas_call(
        hidden_kernel,
        in_specs=[whole] * (1 + len(pieces)),
        out_specs=whole,
        out_shape=jax.ShapeDtypeStruct((count, len(pieces) * LANES), rows.dtype),
        compiler_params=pltpu.CompilerParams(vmem_limit_bytes=GRANT),
        cost_estimate=cost(4 * count * width * share * len(pieces), rows, *pieces),
        name="hidden_units",
    )(rows, *pieces)


def finish_kernel(core_ref, spots_ref, x_ref, early_ref, late_ref, own_ref, other_ref, *refs):
    weights, (below_own, below_other, first_ref, rest_ref, held, sems) = refs[:-6], refs[-6:]
    pieces, share, width = held.shape
    half = width // 2
    near = pl.ds(pl.multiple_of(core_ref[0] * half, half), half)
    distant = pl.ds(pl.multiple_of(half - core_ref[0] * half, half), half)
    copies = [
        pltpu.make_async_copy(ref.at[0], held.at[k], sems.at[k]) for k, ref in enumerate(weights)
    ]
    last = pieces - 1
    copies += [
        pltpu.make_async_copy(below_own.at[0], held.at[last, :, near], sems.at[last]),
        pltpu.make_async_copy(below_other.at[0], held.at[last, :, distant], sems.at[last + 1]),
    ]
    for copy in copies:
        copy.start()
    units = activate(
        x_ref,
        [
            (near, own_ref[...].reshape(2 * share, half)),
            (distant, other_ref[...].reshape(2 * share, half)),
        ],
        share,
    )
    blank = jnp.zeros((units.shape[0], LANES - share), units.dtype)
    hidden = jnp.concatenate([early_ref[...], late_ref[...], units, blank], axis=1)
    for copy in copies:
        copy.wait()
    gap = jnp.zeros((LANES - share, TILE), units.dtype)
    cut = first_ref.shape[3]
    for start in range(0, width, TILE):
        parts = []
        for k in range(pieces):
            parts += [held[k, :, start : start + TILE], gap]
        total = jnp.dot(
            hidden, jnp.concatenate(parts, axis=0), preferred_element_type=jnp.float32
        ).astype(units.dtype)
        for k in range(SIDE * SIDE):
            value = total[k * CAP : (k + 1) * CAP]
            across, along = spots_ref[0, k], spots_ref[1, k]
            if start < cut:
                first_ref[along, across, :, start : start + TILE] = value
            else:
                rest_ref[across, along, :, start - cut : start - cut + TILE] = value


def finish(core, spots, rows, early, late, halves, pieces, below):
    count, width = rows.shape
    share = pieces[0].shape[1]
    whole = pl.BlockSpec(memory_space=pltpu.VMEM)
    scalars = pl.BlockSpec(memory_space=pltpu.SMEM)
    anywhere = pl.BlockSpec(memory_space=pltpu.HBM)
    number = len(pieces) + 1
    return pl.pallas_call(
        finish_kernel,
        in_specs=[scalars] * 2 + [whole] * 5 + [anywhere] * (number + 1),
        out_specs=[whole] * 2,
        out_shape=[
            jax.ShapeDtypeStruct((SIDE, SIDE, CAP, columns), rows.dtype)
            for columns in (Y_FIRST, width - Y_FIRST)
        ],
        scratch_shapes=[
            pltpu.VMEM((number, share, width), rows.dtype),
            pltpu.SemaphoreType.DMA((number + 1,)),
        ],
        compiler_params=pltpu.CompilerParams(vmem_limit_bytes=GRANT),
        cost_estimate=cost(2 * count * width * share * (number + 2), rows, rows, *pieces),
        name="finish_terms",
    )(core, spots, rows, early, late, *halves, *pieces, *below)


def along_z(value, depth):
    pairs = [(z, (z + 1) % depth) for z in range(depth)]
    pairs += [(depth + z, depth + (z - 1) % depth) for z in range(depth)]
    return lax.ppermute(value, ("c", "z"), pairs)


def swapped(value):
    return lax.ppermute(value, "c", [(0, 1), (1, 0)])


def along_x(value, step):
    places = [(x % 2) * 2 + x // 2 for x in range(SIDE)]
    return lax.ppermute(
        value, ("xl", "xh"), [(places[x], places[(x + step) % SIDE]) for x in range(SIDE)]
    )


def along_y(value, step):
    return lax.ppermute(value, "y", [(y, (y + step) % SIDE) for y in range(SIDE)])


def both(first, second):
    return jnp.concatenate([first, second], axis=0)


def body(tokens, expert_ids, route_logits, w_gate, w_up, w_down):
    width = tokens.shape[1]
    chips = lax.axis_size(PLANE)
    depth = lax.axis_size("z")
    share = w_gate.shape[1] // 4
    xl, xh, y = lax.axis_index("xl"), lax.axis_index("xh"), lax.axis_index("y")
    core = lax.axis_index("c").astype(jnp.int32)
    at = jnp.stack([y % 2, xl * 2 + y // 2]).astype(jnp.int32)
    sources = jnp.arange(chips, dtype=jnp.int32)
    across = (sources % 2 * 2 + sources // 8 - (xh * 2 + xl)) % SIDE
    along = (sources // 2 % SIDE - y) % SIDE
    spots = jnp.stack([across, along])

    gate_up, below = pack(at, w_gate, w_up, w_down, share)
    picked, place = pick(expert_ids, route_logits, tokens, chips)
    rows = lax.all_to_all(picked, PLANE, 0, 0).reshape(chips * CAP, width)

    firsts, lasts = [gate_up], [below]
    for _ in range(depth // 2 - 1):
        gate_up, below = along_z(gate_up, depth), along_z(below, depth)
        gate_up, below = lax.optimization_barrier((gate_up, below))
        firsts += [gate_up, swapped(gate_up)]
        lasts += [below, swapped(below)]

    gate_up, below = halve(core.reshape(1), gate_up, below)
    gate_up, below = along_z(gate_up, depth), along_z(below, depth)
    early = hidden_units(rows, firsts[:EARLY])
    late = hidden_units(rows, firsts[EARLY:])
    gate_up, below, early = lax.optimization_barrier((gate_up, below, early))
    first, rest = finish(
        core.reshape(1),
        spots,
        rows,
        early,
        late,
        (gate_up, swapped(gate_up)),
        lasts,
        (below, swapped(below)),
    )
    return mix(at, place, home_y_first(first), home_x_first(rest))


def home_x_first(terms):
    right, left = along_x(terms[2, :2], 1), along_x(terms[2, 2:], -1)
    right = along_x(both(terms[1, :2] + right, terms[1, 2:]), 1)
    left = along_x(both(terms[3, :2], terms[3, 2:] + left), -1)
    mine = terms[0] + right + left
    return [mine[0], along_y(mine[2], 2), along_y(mine[1], 1), along_y(mine[3], -1)]


def home_y_first(terms):
    over, up, down = along_y(terms[2], 2), along_y(terms[1], 1), along_y(terms[3], -1)
    same, crossed = terms[0] + over, up + down
    pairs = [jnp.stack([same[k], crossed[k]]) for k in range(SIDE)]
    return [pairs[0]] + [along_x(pairs[k], k) for k in range(1, SIDE)]


def both(first, second):
    return jnp.concatenate([first, second], axis=0)


def mix_kernel(at_ref, place_ref, *refs):
    near, far, out_ref = refs[:SIDE], refs[SIDE:-1], refs[-1]
    role = at_ref[0]
    places = [place_ref[role], place_ref[1 - role]]

    def spread(values):
        total = None
        for place, value in zip(places, values):
            high = value.astype(jnp.bfloat16)
            low = (value - high.astype(jnp.float32)).astype(jnp.bfloat16)
            part = jnp.dot(place, high, preferred_element_type=jnp.float32) + jnp.dot(
                place, low, preferred_element_type=jnp.float32
            )
            total = part if total is None else total + part
        return total.astype(out_ref.dtype)

    def wide(value):
        return value.astype(jnp.float32)

    cut = near[0].shape[2]
    out_ref[:, :cut] = spread([sum(wide(ref[e]) for ref in near) for e in range(EXPERTS)])
    out_ref[:, cut:] = spread(
        [wide(far[2 * e][...]) + wide(far[2 * e + 1][...]) for e in range(EXPERTS)]
    )


def mix(at, place, near, far):
    rows = place.shape[1]
    width = near[0].shape[-1] + far[0].shape[-1]
    return pl.pallas_call(
        mix_kernel,
        in_specs=[pl.BlockSpec(memory_space=pltpu.SMEM)]
        + [pl.BlockSpec(memory_space=pltpu.VMEM)] * (1 + len(near) + len(far)),
        out_specs=pl.BlockSpec(memory_space=pltpu.VMEM),
        out_shape=jax.ShapeDtypeStruct((rows, width), jnp.bfloat16),
        compiler_params=pltpu.CompilerParams(vmem_limit_bytes=GRANT),
        name="mix_terms",
    )(at, place, *near, *far)


def solution(mesh):
    fine = Mesh(mesh.devices.reshape(2, 4, 2, 8, 2), ("xl", "y", "c", "z", "xh"))
    tokens = P(("xl", "y", "c", "z", "xh"), None)
    weights = P(None, ("z", "xh"), None)
    return jax.shard_map(
        body,
        mesh=fine,
        in_specs=(tokens,) * 3 + (weights,) * 3,
        out_specs=tokens,
        check_vma=False,
    )
```
